32 devices in a mesh: ent: 8 (over z, y), rep: 4 (over x, core).
Axes of the slice: x: 2, y: 2, z: 4, core: 2. Of those that a mesh axis runs over, the one named last changes fastest.
Arguments:
- table: float32 [32768, 256], P('ent'), may hold values from -6.1 to 6.1
- relations: float32 [824, 256], P('rep'), may hold values from -4 to 4
- anchor: int32 [2048], P('rep'), may hold values from 0 to 32767
- rel_one: int32 [2048], P('rep'), may hold values from 0 to 823
- rel_two: int32 [2048], P('rep'), may hold values from 0 to 823
Outputs:
- log_answer: float32 [2048, 32768], P('rep', 'ent')
The draws below stay inside these ranges and needn't reach their ends.
All inputs are finite; a program needn't handle non-finite values.
Results may differ from the reference program's by a relative error of at most 0.00018.
Values sent between devices are 32-bit elements; how exact they have to be, the bound alone decides.
A program may use at most 128 MiB of HBM per device.

```python
import math
import jax
import jax.numpy as jnp
from jax import lax

RANK = 128
NREL = 824
ENTITIES = 32768
QUERIES = 2048


def draw_table(key, part):
    first = jax.random.fold_in(jax.random.fold_in(key, 11), 0)
    base = jnp.clip(jax.random.normal(first, (ENTITIES, 2 * RANK), jnp.float32), -6.0, 6.0)
    return (0.35 * base).astype(jnp.float32)


def touch_ends(values, stream_key, low, largest):
    longest = values.shape.index(max(values.shape))
    spots = []
    for shift in (0, 1):
        where = [jax.random.randint(jax.random.fold_in(stream_key, axis), (), 0, length) for axis, length in enumerate(values.shape)]
        where[longest] = (where[longest] + shift) % values.shape[longest]
        spots.append(tuple(where))
    return values.at[spots[0]].set(low).at[spots[1]].set(largest)


def block_scale(own_key, extent, pieces, low, largest):
    level, own = 1.0, jax.random.fold_in(own_key, 6)
    for axis_at, parts in pieces:
        steps = jnp.exp(jax.random.uniform(jax.random.fold_in(own, axis_at), (parts,), jnp.float32, low / len(pieces), largest / len(pieces)))
        level = level * jnp.repeat(steps, extent[axis_at] // parts).reshape([-1 if axis == axis_at else 1 for axis in range(len(extent))])
    return level


def normal_values(stream_key, dims, deviation, reach, cuts=(), held_as=jnp.bfloat16):
    gain = block_scale(stream_key, dims, cuts, -0.22, 0.18) if cuts else 1.0
    array = jax.random.normal(stream_key, dims, jnp.float32) * deviation * gain
    return jnp.minimum(jnp.maximum(array, -reach), reach).astype(held_as)


def setup_inputs(seed: int = 0) -> dict:
    key_of = jax.random.split(jax.random.key(seed), 6)
    return {
        "table": draw_table(jax.random.fold_in(key_of[5], 71), 0),
        "relations": normal_values(key_of[1], (NREL, 2 * RANK), 1.0, 4.0, ((0, 4),), jnp.float32),
        "anchor": touch_ends(jax.random.randint(key_of[2], (QUERIES,), 0, ENTITIES), jax.random.fold_in(key_of[2], 1), 0, ENTITIES - 1).astype(jnp.int32),
        "rel_one": touch_ends(jax.random.randint(key_of[3], (QUERIES,), 0, NREL), jax.random.fold_in(key_of[3], 1), 0, NREL - 1).astype(jnp.int32),
        "rel_two": touch_ends(jax.random.randint(key_of[4], (QUERIES,), 0, NREL), jax.random.fold_in(key_of[4], 1), 0, NREL - 1).astype(jnp.int32),
    }


def cmul(left, right):
    half = left.shape[1] // 2
    lre, lim = left[:, :half], left[:, half:]
    rre, rim = right[:, :half], right[:, half:]
    return jnp.concatenate([lre * rre - lim * rim, lre * rim + lim * rre], axis=1)


def reference(table, relations, anchor, rel_one, rel_two):
    highest = lax.Precision.HIGHEST
    query_one = cmul(table[anchor], relations[rel_one])
    rel_second = relations[rel_two]
    block = math.gcd(QUERIES, 128)
    count = QUERIES // block

    def one_block(pair):
        query, second = pair
        scores = jnp.dot(query, table.T, precision=highest, preferred_element_type=jnp.float32)
        peak = jnp.max(scores, axis=1, keepdims=True)
        weights = jnp.exp(scores - peak)
        prob = weights / jnp.sum(weights, axis=1, keepdims=True)
        expected = jnp.dot(prob, table, precision=highest, preferred_element_type=jnp.float32)
        query_two = cmul(expected, second)
        scores_two = jnp.dot(query_two, table.T, precision=highest, preferred_element_type=jnp.float32)
        peak_two = jnp.max(scores_two, axis=1, keepdims=True)
        shifted = scores_two - peak_two
        return shifted - jnp.log(jnp.sum(jnp.exp(shifted), axis=1, keepdims=True))

    result = lax.map(one_block, (query_one.reshape(count, block, -1), rel_second.reshape(count, block, -1)))
    return result.reshape(QUERIES, ENTITIES)
```

```python
import functools

import jax
import jax.numpy as jnp
from jax import lax
from jax.experimental import pallas as pl
from jax.experimental.pallas import tpu as pltpu
from jax.sharding import PartitionSpec as P

MESH = pl.DeviceIdType.MESH
F32, BF16 = jnp.float32, jnp.bfloat16


def cmul(left, right):
    half = left.shape[1] // 2
    lre, lim = left[:, :half], left[:, half:]
    rre, rim = right[:, :half], right[:, half:]
    return jnp.concatenate([lre * rre - lim * rim, lre * rim + lim * rre], axis=1)


def halves(x):
    high = x.astype(BF16)
    return high, (x - high.astype(F32)).astype(BF16)


def dot(a, b, contract):
    return lax.dot_general(a, b, (contract, ((), ())), preferred_element_type=F32)


def dot3(a, b, contract):
    return dot(a[0], b[0], contract) + (dot(a[0], b[1], contract) + dot(a[1], b[0], contract))


NT = ((1,), (1,))
NN = ((1,), (0,))


def kernel(
    n, m, tile, block,
    table, relations, anchor, rel_one, rel_two,
    scores_out, lse_out,
    t_hi, t_lo, scores, asend, arecv, rels, r1, r2, acc, q1, q2, csend, crecv, erecv, esend,
    sa, ra, sr, rr, sb, rb, sc, rc, sd, rd, se, re, so,
):
    me, mine = lax.axis_index("ent"), lax.axis_index("rep")
    rows, width = q1.shape
    chunk = rows // n
    ents = table.shape[0]
    start = me * ents
    nrel = relations.shape[0]

    def to(k):
        return lax.rem(me + k, n)

    def source(k):
        return lax.rem(me - k + n, n)

    def at(d):
        return pl.ds(pl.multiple_of(d * chunk, 8), chunk)

    def ent_copy(src, dst, send, recv, k):
        return pltpu.make_async_remote_copy(
            src_ref=src, dst_ref=dst, send_sem=send.at[k], recv_sem=recv.at[k],
            device_id={"ent": to(k)}, device_id_type=MESH,
        )

    def rel_copy(j, slot):
        return pltpu.make_async_remote_copy(
            src_ref=relations, dst_ref=rels.at[slot], send_sem=sr.at[j], recv_sem=rr.at[j],
            device_id={"rep": lax.rem(mine + j, m)}, device_id_type=MESH,
        )

    def each(body):
        lax.fori_loop(1, n, lambda k, c: (body(k), c)[1], 0)

    barrier = pltpu.get_barrier_semaphore()
    each(lambda k: pl.semaphore_signal(barrier, inc=1, device_id={"ent": to(k)}, device_id_type=MESH))
    for j in range(1, m):
        pl.semaphore_signal(barrier, inc=1, device_id={"rep": lax.rem(mine + j, m)}, device_id_type=MESH)

    def gather(d):
        def one(i, c):
            row = d * chunk + i
            off = anchor[row] - start
            inside = jnp.logical_and(off >= 0, off < ents)
            value = table[pl.ds(jnp.clip(off, 0, ents - 1), 1), :]
            asend[pl.ds(row, 1), :] = jnp.where(inside, value, 0.0)
            return c
        lax.fori_loop(0, chunk, one, 0, unroll=8)

    pl.semaphore_wait(barrier, n - 1 + m - 1)
    for j in range(1, m):
        rel_copy(j, mine).start()

    def a_copy(k):
        return ent_copy(asend.at[at(to(k))], arecv.at[k], sa, ra, k)

    def a_step(k):
        gather(to(k))
        a_copy(k).start()

    each(a_step)
    gather(me)
    rels[mine] = relations[...]

    def split(i, c):
        part = pl.ds(pl.multiple_of(i * 256, 256), 256)
        t_hi[part, :], t_lo[part, :] = halves(table[part, :])
        return c
    lax.fori_loop(0, ents // 256, split, 0)

    for j in range(1, m):
        rel_copy(j, lax.rem(mine - j + m, m)).wait_recv()

    def pick(i, c):
        first, second = rel_one[me * chunk + i], rel_two[me * chunk + i]
        r1[pl.ds(i, 1), :] = rels[first // nrel, pl.ds(lax.rem(first, nrel), 1), :]
        r2[pl.ds(i, 1), :] = rels[second // nrel, pl.ds(lax.rem(second, nrel), 1), :]
        return c
    lax.fori_loop(0, chunk, pick, 0, unroll=8)

    acc[...] = asend[at(me), :]

    def a_sum(k):
        a_copy(k).wait_recv()
        acc[...] += arecv[k]
    each(a_sum)
    q1[at(me), :] = cmul(acc[...], r1[...])

    def share(q, send, recv):
        each(lambda k: ent_copy(q.at[at(me)], q.at[at(me)], send, recv, k).start())

    def arrived(q, send, recv):
        each(lambda k: ent_copy(q.at[at(me)], q.at[at(source(k))], send, recv, k).wait_recv())

    share(q1, sb, rb)
    arrived(q1, sb, rb)

    def score(q, b):
        part = slice(b * block, (b + 1) * block)
        query = halves(q[part, :])
        peak = None
        for t in range(ents // tile):
            cols = slice(t * tile, (t + 1) * tile)
            s = dot3(query, (t_hi[cols, :], t_lo[cols, :]), NT)
            scores[part, cols] = s
            top = jnp.max(s, axis=1, keepdims=True)
            peak = top if peak is None else jnp.maximum(peak, top)
        return part, peak

    def c_copy(k):
        return ent_copy(csend.at[at(to(k))], crecv.at[k], sc, rc, k)

    for b in range(rows // block):
        part, peak = score(q1, b)
        total = jnp.zeros((block, 1), F32)
        summed = jnp.zeros((block, width), F32)
        for t in range(ents // tile):
            cols = slice(t * tile, (t + 1) * tile)
            w = jnp.exp(scores[part, cols] - peak)
            total += jnp.sum(w, axis=1, keepdims=True)
            summed += dot3(halves(w), (t_hi[cols, :], t_lo[cols, :]), NN)
        csend[part, :width] = summed
        lane = lax.broadcasted_iota(jnp.int32, (block, 128), 1)
        csend[part, width:] = jnp.where(lane < 64, peak, total)
    each(lambda k: c_copy(k).start())

    crecv[0] = csend[at(me), :]
    each(lambda k: c_copy(k).wait_recv())
    peak = lax.fori_loop(
        1, n, lambda k, p: jnp.maximum(p, crecv[k, :, width : width + 1]), crecv[0, :, width : width + 1]
    )
    acc[...] = jnp.zeros_like(acc)

    def c_sum(k, total):
        scale = jnp.exp(crecv[k, :, width : width + 1] - peak)
        acc[...] += crecv[k, :, :width] * scale
        return total + crecv[k, :, width + 127 : width + 128] * scale
    total = lax.fori_loop(0, n, c_sum, jnp.zeros((chunk, 1), F32))
    q2[at(me), :] = cmul(acc[...] / total, r2[...])
    share(q2, sd, rd)
    arrived(q2, sd, rd)

    def out_copy(b):
        part = pl.ds(b * block, block)
        return pltpu.make_async_copy(scores.at[part], scores_out.at[part], so.at[b])

    for b in range(rows // block):
        part, peak = score(q2, b)
        out_copy(b).start()
        mass = jnp.zeros((block, 1), F32)
        for t in range(ents // tile):
            cols = slice(t * tile, (t + 1) * tile)
            mass += jnp.sum(jnp.exp(scores[part, cols] - peak), axis=1, keepdims=True)
        lse = jnp.broadcast_to(peak + jnp.log(mass), (block, 128))
        esend[:, part] = lse.T[:8, :]

    def e_copy(k):
        return ent_copy(esend, erecv.at[k], se, re, k)
    each(lambda k: e_copy(k).start())
    erecv[0] = esend[...]
    each(lambda k: e_copy(k).wait_recv())
    top = lax.fori_loop(1, n, lambda k, p: jnp.maximum(p, erecv[k]), erecv[0])
    mass = lax.fori_loop(0, n, lambda k, c: c + jnp.exp(erecv[k] - top), jnp.zeros_like(top))
    lse_out[...] = top + jnp.log(mass)

    for j in range(1, m):
        rel_copy(j, mine).wait_send()

    def drain(k):
        a_copy(k).wait_send()
        ent_copy(q1.at[at(me)], q1.at[at(me)], sb, rb, k).wait_send()
        c_copy(k).wait_send()
        ent_copy(q2.at[at(me)], q2.at[at(me)], sd, rd, k).wait_send()
        e_copy(k).wait_send()
    each(drain)
    for b in range(rows // block):
        out_copy(b).wait()


def solution(mesh):
    n, m = mesh.shape["ent"], mesh.shape["rep"]

    def on_device(table, relations, anchor, rel_one, rel_two):
        ents, width = table.shape
        rows = anchor.shape[0]
        chunk = rows // n
        block = min(rows, 256)
        tile = min(ents, 512)
        vmem, smem = pl.BlockSpec(memory_space=pltpu.VMEM), pl.BlockSpec(memory_space=pltpu.SMEM)
        dma = pltpu.SemaphoreType.DMA
        scores, lse = pl.pallas_call(
            functools.partial(kernel, n, m, tile, block),
            out_shape=(
                jax.ShapeDtypeStruct((rows, ents), F32),
                jax.ShapeDtypeStruct((8, rows), F32),
            ),
            in_specs=[vmem, vmem, smem, smem, smem],
            out_specs=(pl.BlockSpec(memory_space=pl.ANY), vmem),
            scratch_shapes=[
                pltpu.VMEM((ents, width), BF16),
                pltpu.VMEM((ents, width), BF16),
                pltpu.VMEM((rows, ents), F32),
                pltpu.VMEM((rows, width), F32),
                pltpu.VMEM((n, chunk, width), F32),
                pltpu.VMEM((m, relations.shape[0], width), F32),
                pltpu.VMEM((chunk, width), F32),
                pltpu.VMEM((chunk, width), F32),
                pltpu.VMEM((chunk, width), F32),
                pltpu.VMEM((rows, width), F32),
                pltpu.VMEM((rows, width), F32),
                pltpu.VMEM((rows, width + 128), F32),
                pltpu.VMEM((n, chunk, width + 128), F32),
                pltpu.VMEM((n, 8, rows), F32),
                pltpu.VMEM((8, rows), F32),
                dma((n,)), dma((n,)), dma((m,)), dma((m,)),
                dma((n,)), dma((n,)), dma((n,)), dma((n,)),
                dma((n,)), dma((n,)), dma((n,)), dma((n,)),
                dma((rows // block,)),
            ],
            compiler_params=pltpu.CompilerParams(
                collective_id=0, has_side_effects=True, vmem_limit_bytes=52 * 1024 * 1024
            ),
            cost_estimate=pl.CostEstimate(
                flops=18 * rows * ents * width, bytes_accessed=4 * rows * ents,
                transcendentals=2 * rows * ents,
            ),
        )(table, relations, anchor, rel_one, rel_two)
        return scores - lse[0][:, None]

    return jax.shard_map(
        on_device,
        mesh=mesh,
        in_specs=(P("ent", None), P("rep", None), P("rep"), P("rep"), P("rep")),
        out_specs=P("rep", "ent"),
        check_vma=False,
    )
```

```python
import functools

import jax
import jax.numpy as jnp
from jax import lax
from jax.experimental import pallas as pl
from jax.experimental.pallas import tpu as pltpu
from jax.sharding import PartitionSpec as P

MESH = pl.DeviceIdType.MESH
F32, BF16 = jnp.float32, jnp.bfloat16


def cmul(left, right):
    half = left.shape[1] // 2
    lre, lim = left[:, :half], left[:, half:]
    rre, rim = right[:, :half], right[:, half:]
    return jnp.concatenate([lre * rre - lim * rim, lre * rim + lim * rre], axis=1)


def halves(x):
    high = x.astype(BF16)
    return high, (x - high.astype(F32)).astype(BF16)


def dot(a, b, contract):
    return lax.dot_general(a, b, (contract, ((), ())), preferred_element_type=F32)


def dot3(a, b, contract):
    return dot(a[0], b[0], contract) + (dot(a[0], b[1], contract) + dot(a[1], b[0], contract))


NT = ((1,), (1,))
NN = ((1,), (0,))


def kernel(
    n, m, tile, block,
    table, relations, anchor, rel_one, rel_two,
    scores_out, lse_out,
    t_hi, t_lo, scores, asend, arecv, rels, r1, r2, acc, q1, q2, csend, crecv, erecv, esend,
    sa, ra, sr, rr, sb, rb, sc, rc, sd, rd, se, re, so,
):
    me, mine = lax.axis_index("ent"), lax.axis_index("rep")
    rows, width = q1.shape
    chunk = rows // n
    ents = table.shape[0]
    start = me * ents
    nrel = relations.shape[0]

    def to(k):
        return lax.rem(me + k, n)

    def source(k):
        return lax.rem(me - k + n, n)

    def at(d):
        return pl.ds(pl.multiple_of(d * chunk, 8), chunk)

    def ent_copy(src, dst, send, recv, k):
        return pltpu.make_async_remote_copy(
            src_ref=src, dst_ref=dst, send_sem=send.at[k], recv_sem=recv.at[k],
            device_id={"ent": to(k)}, device_id_type=MESH,
        )

    def rel_copy(j, slot):
        return pltpu.make_async_remote_copy(
            src_ref=relations, dst_ref=rels.at[slot], send_sem=sr.at[j], recv_sem=rr.at[j],
            device_id={"rep": lax.rem(mine + j, m)}, device_id_type=MESH,
        )

    def each(body):
        lax.fori_loop(1, n, lambda k, c: (body(k), c)[1], 0)

    per = block // chunk
    blocks = rows // block
    near = me // per

    def among(first, count, body):
        def one(i, c):
            k = lax.rem(lax.rem(first + i, n) - me + n, n)

            @pl.when(k != 0)
            def _():
                body(k)
            return c
        lax.fori_loop(0, count, one, 0)

    def far_first(body):
        among((near + 1) * per, n, body)

    barrier = pltpu.get_barrier_semaphore()
    each(lambda k: pl.semaphore_signal(barrier, inc=1, device_id={"ent": to(k)}, device_id_type=MESH))
    for j in range(1, m):
        pl.semaphore_signal(barrier, inc=1, device_id={"rep": lax.rem(mine + j, m)}, device_id_type=MESH)

    def gather(d):
        def one(i, c):
            row = d * chunk + i
            off = anchor[row] - start
            inside = jnp.logical_and(off >= 0, off < ents)
            value = table[pl.ds(jnp.clip(off, 0, ents - 1), 1), :]
            asend[pl.ds(row, 1), :] = jnp.where(inside, value, 0.0)
            return c
        lax.fori_loop(0, chunk, one, 0, unroll=8)

    pl.semaphore_wait(barrier, n - 1 + m - 1)
    for j in range(1, m):
        rel_copy(j, mine).start()

    def a_copy(k):
        return ent_copy(asend.at[at(to(k))], arecv.at[k], sa, ra, k)

    def a_step(k):
        gather(to(k))
        a_copy(k).start()

    far_first(a_step)
    gather(me)
    rels[mine] = relations[...]

    def split(i, c):
        part = pl.ds(pl.multiple_of(i * 256, 256), 256)
        t_hi[part, :], t_lo[part, :] = halves(table[part, :])
        return c
    lax.fori_loop(0, ents // 256, split, 0)

    for j in range(1, m):
        rel_copy(j, lax.rem(mine - j + m, m)).wait_recv()

    def pick(i, c):
        first, second = rel_one[me * chunk + i], rel_two[me * chunk + i]
        r1[pl.ds(i, 1), :] = rels[first // nrel, pl.ds(lax.rem(first, nrel), 1), :]
        r2[pl.ds(i, 1), :] = rels[second // nrel, pl.ds(lax.rem(second, nrel), 1), :]
        return c
    lax.fori_loop(0, chunk, pick, 0, unroll=8)

    acc[...] = asend[at(me), :]

    def a_sum(k):
        a_copy(k).wait_recv()
        acc[...] += arecv[k]
    each(a_sum)
    q1[at(me), :] = cmul(acc[...], r1[...])

    def share(q, send, recv):
        far_first(lambda k: ent_copy(q.at[at(me)], q.at[at(me)], send, recv, k).start())

    def arrived(q, send, recv, b):
        def one(i, c):
            s = b * per + i
            k = lax.rem(me - s + n, n)

            @pl.when(k != 0)
            def _():
                ent_copy(q.at[at(me)], q.at[at(s)], send, recv, k).wait_recv()
            return c
        lax.fori_loop(0, per, one, 0)

    def place(step):
        return lax.rem(near + step, blocks)

    share(q1, sb, rb)

    def score(q, b):
        part = pl.ds(pl.multiple_of(b * block, block), block)
        query = halves(q[part, :])
        peak = None
        for t in range(ents // tile):
            cols = slice(t * tile, (t + 1) * tile)
            s = dot3(query, (t_hi[cols, :], t_lo[cols, :]), NT)
            scores[part, cols] = s
            top = jnp.max(s, axis=1, keepdims=True)
            peak = top if peak is None else jnp.maximum(peak, top)
        return part, peak

    def c_copy(k):
        return ent_copy(csend.at[at(to(k))], crecv.at[k], sc, rc, k)

    for step in range(blocks):
        b = place(step)
        arrived(q1, sb, rb, b)
        part, peak = score(q1, b)
        total = jnp.zeros((block, 1), F32)
        summed = jnp.zeros((block, width), F32)
        for t in range(ents // tile):
            cols = slice(t * tile, (t + 1) * tile)
            w = jnp.exp(scores[part, cols] - peak)
            total += jnp.sum(w, axis=1, keepdims=True)
            summed += dot3(halves(w), (t_hi[cols, :], t_lo[cols, :]), NN)
        csend[part, :width] = summed
        lane = lax.broadcasted_iota(jnp.int32, (block, 128), 1)
        csend[part, width:] = jnp.where(lane < 64, peak, total)
        among(b * per, per, lambda k: c_copy(k).start())

    crecv[0] = csend[at(me), :]
    each(lambda k: c_copy(k).wait_recv())
    peak = lax.fori_loop(
        1, n, lambda k, p: jnp.maximum(p, crecv[k, :, width : width + 1]), crecv[0, :, width : width + 1]
    )
    acc[...] = jnp.zeros_like(acc)

    def c_sum(k, total):
        scale = jnp.exp(crecv[k, :, width : width + 1] - peak)
        acc[...] += crecv[k, :, :width] * scale
        return total + crecv[k, :, width + 127 : width + 128] * scale
    total = lax.fori_loop(0, n, c_sum, jnp.zeros((chunk, 1), F32))
    q2[at(me), :] = cmul(acc[...] / total, r2[...])
    share(q2, sd, rd)

    def out_copy(b):
        part = pl.ds(pl.multiple_of(b * block, block), block)
        return pltpu.make_async_copy(scores.at[part], scores_out.at[part], so.at[b])

    for step in range(blocks):
        b = place(step)
        arrived(q2, sd, rd, b)
        part, peak = score(q2, b)
        out_copy(b).start()
        mass = jnp.zeros((block, 1), F32)
        for t in range(ents // tile):
            cols = slice(t * tile, (t + 1) * tile)
            mass += jnp.sum(jnp.exp(scores[part, cols] - peak), axis=1, keepdims=True)
        lse = jnp.broadcast_to(peak + jnp.log(mass), (block, 128))
        esend[:, part] = lse.T[:8, :]

    def e_copy(k):
        return ent_copy(esend, erecv.at[k], se, re, k)
    each(lambda k: e_copy(k).start())
    erecv[0] = esend[...]
    each(lambda k: e_copy(k).wait_recv())
    top = lax.fori_loop(1, n, lambda k, p: jnp.maximum(p, erecv[k]), erecv[0])
    mass = lax.fori_loop(0, n, lambda k, c: c + jnp.exp(erecv[k] - top), jnp.zeros_like(top))
    lse_out[...] = top + jnp.log(mass)

    for j in range(1, m):
        rel_copy(j, mine).wait_send()

    def drain(k):
        a_copy(k).wait_send()
        ent_copy(q1.at[at(me)], q1.at[at(me)], sb, rb, k).wait_send()
        c_copy(k).wait_send()
        ent_copy(q2.at[at(me)], q2.at[at(me)], sd, rd, k).wait_send()
        e_copy(k).wait_send()
    each(drain)
    for b in range(rows // block):
        out_copy(b).wait()


def solution(mesh):
    n, m = mesh.shape["ent"], mesh.shape["rep"]

    def on_device(table, relations, anchor, rel_one, rel_two):
        ents, width = table.shape
        rows = anchor.shape[0]
        chunk = rows // n
        block = min(rows, 256)
        tile = min(ents, 512)
        vmem, smem = pl.BlockSpec(memory_space=pltpu.VMEM), pl.BlockSpec(memory_space=pltpu.SMEM)
        dma = pltpu.SemaphoreType.DMA
        scores, lse = pl.pallas_call(
            functools.partial(kernel, n, m, tile, block),
            out_shape=(
                jax.ShapeDtypeStruct((rows, ents), F32),
                jax.ShapeDtypeStruct((8, rows), F32),
            ),
            in_specs=[vmem, vmem, smem, smem, smem],
            out_specs=(pl.BlockSpec(memory_space=pl.ANY), vmem),
            scratch_shapes=[
                pltpu.VMEM((ents, width), BF16),
                pltpu.VMEM((ents, width), BF16),
                pltpu.VMEM((rows, ents), F32),
                pltpu.VMEM((rows, width), F32),
                pltpu.VMEM((n, chunk, width), F32),
                pltpu.VMEM((m, relations.shape[0], width), F32),
                pltpu.VMEM((chunk, width), F32),
                pltpu.VMEM((chunk, width), F32),
                pltpu.VMEM((chunk, width), F32),
                pltpu.VMEM((rows, width), F32),
                pltpu.VMEM((rows, width), F32),
                pltpu.VMEM((rows, width + 128), F32),
                pltpu.VMEM((n, chunk, width + 128), F32),
                pltpu.VMEM((n, 8, rows), F32),
                pltpu.VMEM((8, rows), F32),
                dma((n,)), dma((n,)), dma((m,)), dma((m,)),
                dma((n,)), dma((n,)), dma((n,)), dma((n,)),
                dma((n,)), dma((n,)), dma((n,)), dma((n,)),
                dma((rows // block,)),
            ],
            compiler_params=pltpu.CompilerParams(
                collective_id=0, has_side_effects=True, vmem_limit_bytes=32 * 1024 * 1024
            ),
            cost_estimate=pl.CostEstimate(
                flops=18 * rows * ents * width, bytes_accessed=4 * rows * ents,
                transcendentals=2 * rows * ents,
            ),
        )(table, relations, anchor, rel_one, rel_two)
        return scores - lse[0][:, None]

    return jax.shard_map(
        on_device,
        mesh=mesh,
        in_specs=(P("ent", None), P("rep", None), P("rep"), P("rep"), P("rep")),
        out_specs=P("rep", "ent"),
        check_vma=False,
    )
```

```python
import functools

import jax
import jax.numpy as jnp
from jax import lax
from jax.experimental import pallas as pl
from jax.experimental.pallas import tpu as pltpu
from jax.sharding import PartitionSpec as P

MESH = pl.DeviceIdType.MESH
F32, BF16 = jnp.float32, jnp.bfloat16


def cmul(left, right):
    half = left.shape[1] // 2
    lre, lim = left[:, :half], left[:, half:]
    rre, rim = right[:, :half], right[:, half:]
    return jnp.concatenate([lre * rre - lim * rim, lre * rim + lim * rre], axis=1)


def halves(x):
    high = x.astype(BF16)
    return high, (x - high.astype(F32)).astype(BF16)


def dot(a, b, contract):
    return lax.dot_general(a, b, (contract, ((), ())), preferred_element_type=F32)


def dot3(a, b, contract):
    return dot(a[0], b[0], contract) + (dot(a[0], b[1], contract) + dot(a[1], b[0], contract))


NT = ((1,), (1,))
NN = ((1,), (0,))


def kernel(
    n, m, tile, block,
    table, relations, anchor, rel_one, rel_two,
    scores_out, lse_out,
    t_hi, t_lo, scores, asend, arecv, rels, r1, r2, acc, q1, q2, csend, crecv, erecv, esend,
    sa, ra, sr, rr, sb, rb, sc, rc, sd, rd, se, re, so,
):
    me, mine = lax.axis_index("ent"), lax.axis_index("rep")
    rows, width = q1.shape
    chunk = rows // n
    ents = table.shape[0]
    start = me * ents
    nrel = relations.shape[0]

    def to(k):
        return lax.rem(me + k, n)

    def source(k):
        return lax.rem(me - k + n, n)

    def at(d):
        return pl.ds(pl.multiple_of(d * chunk, 8), chunk)

    def ent_copy(src, dst, send, recv, k):
        return pltpu.make_async_remote_copy(
            src_ref=src, dst_ref=dst, send_sem=send.at[k], recv_sem=recv.at[k],
            device_id={"ent": to(k)}, device_id_type=MESH,
        )

    def rel_copy(j, slot):
        return pltpu.make_async_remote_copy(
            src_ref=relations, dst_ref=rels.at[slot], send_sem=sr.at[j], recv_sem=rr.at[j],
            device_id={"rep": lax.rem(mine + j, m)}, device_id_type=MESH,
        )

    def each(body):
        lax.fori_loop(1, n, lambda k, c: (body(k), c)[1], 0)

    per = block // chunk
    blocks = rows // block
    near = me // per

    def among(first, count, body):
        def one(i, c):
            k = lax.rem(lax.rem(first + i, n) - me + n, n)

            @pl.when(k != 0)
            def _():
                body(k)
            return c
        lax.fori_loop(0, count, one, 0)

    def far_first(body):
        among((near + 1) * per, n, body)

    barrier = pltpu.get_barrier_semaphore()
    each(lambda k: pl.semaphore_signal(barrier, inc=1, device_id={"ent": to(k)}, device_id_type=MESH))
    for j in range(1, m):
        pl.semaphore_signal(barrier, inc=1, device_id={"rep": lax.rem(mine + j, m)}, device_id_type=MESH)

    def gather(d):
        def one(i, c):
            row = d * chunk + i
            off = anchor[row] - start
            inside = jnp.logical_and(off >= 0, off < ents)
            value = table[pl.ds(jnp.clip(off, 0, ents - 1), 1), :]
            asend[pl.ds(row, 1), :] = jnp.where(inside, value, 0.0)
            return c
        lax.fori_loop(0, chunk, one, 0, unroll=8)

    pl.semaphore_wait(barrier, n - 1 + m - 1)
    for j in range(1, m):
        rel_copy(j, mine).start()

    def a_copy(k):
        return ent_copy(asend.at[at(to(k))], arecv.at[k], sa, ra, k)

    def a_step(k):
        gather(to(k))
        a_copy(k).start()

    far_first(a_step)
    gather(me)
    rels[mine] = relations[...]

    def split(i, c):
        part = pl.ds(pl.multiple_of(i * 256, 256), 256)
        t_hi[part, :], t_lo[part, :] = halves(table[part, :])
        return c
    lax.fori_loop(0, ents // 256, split, 0)

    for j in range(1, m):
        rel_copy(j, lax.rem(mine - j + m, m)).wait_recv()

    def pick(i, c):
        first, second = rel_one[me * chunk + i], rel_two[me * chunk + i]
        r1[pl.ds(i, 1), :] = rels[first // nrel, pl.ds(lax.rem(first, nrel), 1), :]
        r2[pl.ds(i, 1), :] = rels[second // nrel, pl.ds(lax.rem(second, nrel), 1), :]
        return c
    lax.fori_loop(0, chunk, pick, 0, unroll=8)

    acc[...] = asend[at(me), :]

    def a_sum(k):
        a_copy(k).wait_recv()
        acc[...] += arecv[k]
    each(a_sum)
    q1[at(me), :] = cmul(acc[...], r1[...])

    def share(q, send, recv):
        far_first(lambda k: ent_copy(q.at[at(me)], q.at[at(me)], send, recv, k).start())

    def arrived(q, send, recv, b):
        def one(i, c):
            s = b * per + i
            k = lax.rem(me - s + n, n)

            @pl.when(k != 0)
            def _():
                ent_copy(q.at[at(me)], q.at[at(s)], send, recv, k).wait_recv()
            return c
        lax.fori_loop(0, per, one, 0)

    def place(step):
        return lax.rem(near + step, blocks)

    share(q1, sb, rb)

    def score(q, b):
        part = pl.ds(pl.multiple_of(b * block, block), block)
        query = halves(q[part, :])
        peak = None
        for t in range(ents // tile):
            cols = slice(t * tile, (t + 1) * tile)
            s = dot3(query, (t_hi[cols, :], t_lo[cols, :]), NT)
            scores[part, cols] = s
            top = jnp.max(s, axis=1, keepdims=True)
            peak = top if peak is None else jnp.maximum(peak, top)
        return part, peak

    def c_copy(k):
        return ent_copy(csend.at[at(to(k))], crecv.at[k], sc, rc, k)

    for step in range(blocks):
        b = place(step)
        arrived(q1, sb, rb, b)
        part, peak = score(q1, b)
        total = jnp.zeros((block, 1), F32)
        summed = jnp.zeros((block, width), F32)
        for t in range(ents // tile):
            cols = slice(t * tile, (t + 1) * tile)
            w = jnp.exp(scores[part, cols] - peak)
            total += jnp.sum(w, axis=1, keepdims=True)
            summed += dot3(halves(w), (t_hi[cols, :], t_lo[cols, :]), NN)
        csend[part, :width] = summed
        lane = lax.broadcasted_iota(jnp.int32, (block, 128), 1)
        csend[part, width:] = jnp.where(lane < 64, peak, total)
        among(b * per, per, lambda k: c_copy(k).start())

    crecv[0] = csend[at(me), :]
    each(lambda k: c_copy(k).wait_recv())
    peak = lax.fori_loop(
        1, n, lambda k, p: jnp.maximum(p, crecv[k, :, width : width + 1]), crecv[0, :, width : width + 1]
    )
    acc[...] = jnp.zeros_like(acc)

    def c_sum(k, total):
        scale = jnp.exp(crecv[k, :, width : width + 1] - peak)
        acc[...] += crecv[k, :, :width] * scale
        return total + crecv[k, :, width + 127 : width + 128] * scale
    total = lax.fori_loop(0, n, c_sum, jnp.zeros((chunk, 1), F32))
    q2[at(me), :] = cmul(acc[...] / total, r2[...])
    share(q2, sd, rd)

    def out_copy(b):
        part = pl.ds(pl.multiple_of(b * block, block), block)
        return pltpu.make_async_copy(scores.at[part], scores_out.at[part], so.at[b])

    for step in range(blocks):
        b = place(step)
        arrived(q2, sd, rd, b)
        part, peak = score(q2, b)
        out_copy(b).start()
        mass = jnp.zeros((block, 1), F32)
        for t in range(ents // tile):
            cols = slice(t * tile, (t + 1) * tile)
            mass += jnp.sum(jnp.exp(scores[part, cols] - peak), axis=1, keepdims=True)
        lse = jnp.broadcast_to(peak + jnp.log(mass), (block, 128))
        esend[:, part] = lse.T[:8, :]

    def e_copy(k):
        return ent_copy(esend, erecv.at[k], se, re, k)
    each(lambda k: e_copy(k).start())
    erecv[0] = esend[...]
    each(lambda k: e_copy(k).wait_recv())
    top = lax.fori_loop(1, n, lambda k, p: jnp.maximum(p, erecv[k]), erecv[0])
    mass = lax.fori_loop(0, n, lambda k, c: c + jnp.exp(erecv[k] - top), jnp.zeros_like(top))
    lse_out[...] = top + jnp.log(mass)

    for j in range(1, m):
        rel_copy(j, mine).wait_send()

    def drain(k):
        a_copy(k).wait_send()
        ent_copy(q1.at[at(me)], q1.at[at(me)], sb, rb, k).wait_send()
        c_copy(k).wait_send()
        ent_copy(q2.at[at(me)], q2.at[at(me)], sd, rd, k).wait_send()
        e_copy(k).wait_send()
    each(drain)
    for b in range(rows // block):
        out_copy(b).wait()


def solution(mesh):
    n, m = mesh.shape["ent"], mesh.shape["rep"]

    def on_device(table, relations, anchor, rel_one, rel_two):
        ents, width = table.shape
        rows = anchor.shape[0]
        chunk = rows // n
        block = min(rows, 512)
        tile = min(ents, 512)
        vmem, smem = pl.BlockSpec(memory_space=pltpu.VMEM), pl.BlockSpec(memory_space=pltpu.SMEM)
        dma = pltpu.SemaphoreType.DMA
        scores, lse = pl.pallas_call(
            functools.partial(kernel, n, m, tile, block),
            out_shape=(
                jax.ShapeDtypeStruct((rows, ents), F32),
                jax.ShapeDtypeStruct((8, rows), F32),
            ),
            in_specs=[vmem, vmem, smem, smem, smem],
            out_specs=(pl.BlockSpec(memory_space=pl.ANY), vmem),
            scratch_shapes=[
                pltpu.VMEM((ents, width), BF16),
                pltpu.VMEM((ents, width), BF16),
                pltpu.VMEM((rows, ents), F32),
                pltpu.VMEM((rows, width), F32),
                pltpu.VMEM((n, chunk, width), F32),
                pltpu.VMEM((m, relations.shape[0], width), F32),
                pltpu.VMEM((chunk, width), F32),
                pltpu.VMEM((chunk, width), F32),
                pltpu.VMEM((chunk, width), F32),
                pltpu.VMEM((rows, width), F32),
                pltpu.VMEM((rows, width), F32),
                pltpu.VMEM((rows, width + 128), F32),
                pltpu.VMEM((n, chunk, width + 128), F32),
                pltpu.VMEM((n, 8, rows), F32),
                pltpu.VMEM((8, rows), F32),
                dma((n,)), dma((n,)), dma((m,)), dma((m,)),
                dma((n,)), dma((n,)), dma((n,)), dma((n,)),
                dma((n,)), dma((n,)), dma((n,)), dma((n,)),
                dma((rows // block,)),
            ],
            compiler_params=pltpu.CompilerParams(
                collective_id=0, has_side_effects=True, vmem_limit_bytes=32 * 1024 * 1024
            ),
            cost_estimate=pl.CostEstimate(
                flops=18 * rows * ents * width, bytes_accessed=4 * rows * ents,
                transcendentals=2 * rows * ents,
            ),
        )(table, relations, anchor, rel_one, rel_two)
        return scores - lse[0][:, None]

    return jax.shard_map(
        on_device,
        mesh=mesh,
        in_specs=(P("ent", None), P("rep", None), P("rep"), P("rep"), P("rep")),
        out_specs=P("rep", "ent"),
        check_vma=False,
    )
```

```python
import functools

import jax
import jax.numpy as jnp
from jax import lax
from jax.experimental import pallas as pl
from jax.experimental.pallas import tpu as pltpu
from jax.sharding import PartitionSpec as P

MESH = pl.DeviceIdType.MESH
F32, BF16 = jnp.float32, jnp.bfloat16


def cmul(left, right):
    half = left.shape[1] // 2
    lre, lim = left[:, :half], left[:, half:]
    rre, rim = right[:, :half], right[:, half:]
    return jnp.concatenate([lre * rre - lim * rim, lre * rim + lim * rre], axis=1)


def halves(x):
    high = x.astype(BF16)
    return high, (x - high.astype(F32)).astype(BF16)


def dot(a, b, contract):
    return lax.dot_general(a, b, (contract, ((), ())), preferred_element_type=F32)


def dot3(a, b, contract):
    left = jnp.concatenate([a[0], a[0], a[1]], axis=contract[0][0])
    right = jnp.concatenate([b[0], b[1], b[0]], axis=contract[1][0])
    return dot(left, right, contract)


NT = ((1,), (1,))
NN = ((1,), (0,))


def kernel(
    n, m, tile, block,
    table, relations, anchor, rel_one, rel_two,
    scores_out, lse_out,
    t_hi, t_lo, scores, asend, arecv, rels, r1, r2, acc, q1, q2, csend, crecv, erecv, esend,
    sa, ra, sr, rr, sb, rb, sc, rc, sd, rd, se, re, so,
):
    me, mine = lax.axis_index("ent"), lax.axis_index("rep")
    rows, width = q1.shape
    chunk = rows // n
    ents = table.shape[0]
    start = me * ents
    nrel = relations.shape[0]

    def to(k):
        return lax.rem(me + k, n)

    def source(k):
        return lax.rem(me - k + n, n)

    def at(d):
        return pl.ds(pl.multiple_of(d * chunk, 8), chunk)

    def ent_copy(src, dst, send, recv, k):
        return pltpu.make_async_remote_copy(
            src_ref=src, dst_ref=dst, send_sem=send.at[k], recv_sem=recv.at[k],
            device_id={"ent": to(k)}, device_id_type=MESH,
        )

    def rel_copy(j, slot):
        return pltpu.make_async_remote_copy(
            src_ref=relations, dst_ref=rels.at[slot], send_sem=sr.at[j], recv_sem=rr.at[j],
            device_id={"rep": lax.rem(mine + j, m)}, device_id_type=MESH,
        )

    def each(body):
        lax.fori_loop(1, n, lambda k, c: (body(k), c)[1], 0)

    per = block // chunk
    blocks = rows // block
    near = me // per

    def among(first, count, body):
        def one(i, c):
            k = lax.rem(lax.rem(first + i, n) - me + n, n)

            @pl.when(k != 0)
            def _():
                body(k)
            return c
        lax.fori_loop(0, count, one, 0)

    def far_first(body):
        among((near + 1) * per, n, body)

    barrier = pltpu.get_barrier_semaphore()
    each(lambda k: pl.semaphore_signal(barrier, inc=1, device_id={"ent": to(k)}, device_id_type=MESH))
    for j in range(1, m):
        pl.semaphore_signal(barrier, inc=1, device_id={"rep": lax.rem(mine + j, m)}, device_id_type=MESH)

    def gather(d):
        def one(i, c):
            row = d * chunk + i
            off = anchor[row] - start
            inside = jnp.logical_and(off >= 0, off < ents)
            value = table[pl.ds(jnp.clip(off, 0, ents - 1), 1), :]
            asend[pl.ds(row, 1), :] = jnp.where(inside, value, 0.0)
            return c
        lax.fori_loop(0, chunk, one, 0, unroll=8)

    pl.semaphore_wait(barrier, n - 1 + m - 1)
    for j in range(1, m):
        rel_copy(j, mine).start()

    def a_copy(k):
        return ent_copy(asend.at[at(to(k))], arecv.at[k], sa, ra, k)

    def a_step(k):
        gather(to(k))
        a_copy(k).start()

    far_first(a_step)
    gather(me)
    rels[mine] = relations[...]

    def split(i, c):
        part = pl.ds(pl.multiple_of(i * 256, 256), 256)
        t_hi[part, :], t_lo[part, :] = halves(table[part, :])
        return c
    lax.fori_loop(0, ents // 256, split, 0)

    for j in range(1, m):
        rel_copy(j, lax.rem(mine - j + m, m)).wait_recv()

    def pick(i, c):
        first, second = rel_one[me * chunk + i], rel_two[me * chunk + i]
        r1[pl.ds(i, 1), :] = rels[first // nrel, pl.ds(lax.rem(first, nrel), 1), :]
        r2[pl.ds(i, 1), :] = rels[second // nrel, pl.ds(lax.rem(second, nrel), 1), :]
        return c
    lax.fori_loop(0, chunk, pick, 0, unroll=8)

    acc[...] = asend[at(me), :]

    def a_sum(k):
        a_copy(k).wait_recv()
        acc[...] += arecv[k]
    each(a_sum)
    q1[at(me), :] = cmul(acc[...], r1[...])

    def share(q, send, recv):
        far_first(lambda k: ent_copy(q.at[at(me)], q.at[at(me)], send, recv, k).start())

    def arrived(q, send, recv, b):
        def one(i, c):
            s = b * per + i
            k = lax.rem(me - s + n, n)

            @pl.when(k != 0)
            def _():
                ent_copy(q.at[at(me)], q.at[at(s)], send, recv, k).wait_recv()
            return c
        lax.fori_loop(0, per, one, 0)

    def place(step):
        return lax.rem(near + step, blocks)

    share(q1, sb, rb)

    def score(q, b):
        part = pl.ds(pl.multiple_of(b * block, block), block)
        query = halves(q[part, :])
        peak = None
        for t in range(ents // tile):
            cols = slice(t * tile, (t + 1) * tile)
            s = dot3(query, (t_hi[cols, :], t_lo[cols, :]), NT)
            scores[part, cols] = s
            top = jnp.max(s, axis=1, keepdims=True)
            peak = top if peak is None else jnp.maximum(peak, top)
        return part, peak

    def c_copy(k):
        return ent_copy(csend.at[at(to(k))], crecv.at[k], sc, rc, k)

    for step in range(blocks):
        b = place(step)
        arrived(q1, sb, rb, b)
        part, peak = score(q1, b)
        total = jnp.zeros((block, 1), F32)
        summed = jnp.zeros((block, width), F32)
        for t in range(ents // tile):
            cols = slice(t * tile, (t + 1) * tile)
            w = jnp.exp(scores[part, cols] - peak)
            total += jnp.sum(w, axis=1, keepdims=True)
            summed += dot3(halves(w), (t_hi[cols, :], t_lo[cols, :]), NN)
        csend[part, :width] = summed
        lane = lax.broadcasted_iota(jnp.int32, (block, 128), 1)
        csend[part, width:] = jnp.where(lane < 64, peak, total)
        among(b * per, per, lambda k: c_copy(k).start())

    crecv[0] = csend[at(me), :]
    each(lambda k: c_copy(k).wait_recv())
    peak = lax.fori_loop(
        1, n, lambda k, p: jnp.maximum(p, crecv[k, :, width : width + 1]), crecv[0, :, width : width + 1]
    )
    acc[...] = jnp.zeros_like(acc)

    def c_sum(k, total):
        scale = jnp.exp(crecv[k, :, width : width + 1] - peak)
        acc[...] += crecv[k, :, :width] * scale
        return total + crecv[k, :, width + 127 : width + 128] * scale
    total = lax.fori_loop(0, n, c_sum, jnp.zeros((chunk, 1), F32))
    q2[at(me), :] = cmul(acc[...] / total, r2[...])
    share(q2, sd, rd)

    def out_copy(b):
        part = pl.ds(pl.multiple_of(b * block, block), block)
        return pltpu.make_async_copy(scores.at[part], scores_out.at[part], so.at[b])

    for step in range(blocks):
        b = place(step)
        arrived(q2, sd, rd, b)
        part, peak = score(q2, b)
        out_copy(b).start()
        mass = jnp.zeros((block, 1), F32)
        for t in range(ents // tile):
            cols = slice(t * tile, (t + 1) * tile)
            mass += jnp.sum(jnp.exp(scores[part, cols] - peak), axis=1, keepdims=True)
        lse = jnp.broadcast_to(peak + jnp.log(mass), (block, 128))
        esend[:, part] = lse.T[:8, :]

    def e_copy(k):
        return ent_copy(esend, erecv.at[k], se, re, k)
    each(lambda k: e_copy(k).start())
    erecv[0] = esend[...]
    each(lambda k: e_copy(k).wait_recv())
    top = lax.fori_loop(1, n, lambda k, p: jnp.maximum(p, erecv[k]), erecv[0])
    mass = lax.fori_loop(0, n, lambda k, c: c + jnp.exp(erecv[k] - top), jnp.zeros_like(top))
    lse_out[...] = top + jnp.log(mass)

    for j in range(1, m):
        rel_copy(j, mine).wait_send()

    def drain(k):
        a_copy(k).wait_send()
        ent_copy(q1.at[at(me)], q1.at[at(me)], sb, rb, k).wait_send()
        c_copy(k).wait_send()
        ent_copy(q2.at[at(me)], q2.at[at(me)], sd, rd, k).wait_send()
        e_copy(k).wait_send()
    each(drain)
    for b in range(rows // block):
        out_copy(b).wait()


def solution(mesh):
    n, m = mesh.shape["ent"], mesh.shape["rep"]

    def on_device(table, relations, anchor, rel_one, rel_two):
        ents, width = table.shape
        rows = anchor.shape[0]
        chunk = rows // n
        block = min(rows, 512)
        tile = min(ents, 512)
        vmem, smem = pl.BlockSpec(memory_space=pltpu.VMEM), pl.BlockSpec(memory_space=pltpu.SMEM)
        dma = pltpu.SemaphoreType.DMA
        scores, lse = pl.pallas_call(
            functools.partial(kernel, n, m, tile, block),
            out_shape=(
                jax.ShapeDtypeStruct((rows, ents), F32),
                jax.ShapeDtypeStruct((8, rows), F32),
            ),
            in_specs=[vmem, vmem, smem, smem, smem],
            out_specs=(pl.BlockSpec(memory_space=pl.ANY), vmem),
            scratch_shapes=[
                pltpu.VMEM((ents, width), BF16),
                pltpu.VMEM((ents, width), BF16),
                pltpu.VMEM((rows, ents), F32),
                pltpu.VMEM((rows, width), F32),
                pltpu.VMEM((n, chunk, width), F32),
                pltpu.VMEM((m, relations.shape[0], width), F32),
                pltpu.VMEM((chunk, width), F32),
                pltpu.VMEM((chunk, width), F32),
                pltpu.VMEM((chunk, width), F32),
                pltpu.VMEM((rows, width), F32),
                pltpu.VMEM((rows, width), F32),
                pltpu.VMEM((rows, width + 128), F32),
                pltpu.VMEM((n, chunk, width + 128), F32),
                pltpu.VMEM((n, 8, rows), F32),
                pltpu.VMEM((8, rows), F32),
                dma((n,)), dma((n,)), dma((m,)), dma((m,)),
                dma((n,)), dma((n,)), dma((n,)), dma((n,)),
                dma((n,)), dma((n,)), dma((n,)), dma((n,)),
                dma((rows // block,)),
            ],
            compiler_params=pltpu.CompilerParams(
                collective_id=0, has_side_effects=True, vmem_limit_bytes=32 * 1024 * 1024
            ),
            cost_estimate=pl.CostEstimate(
                flops=18 * rows * ents * width, bytes_accessed=4 * rows * ents,
                transcendentals=2 * rows * ents,
            ),
        )(table, relations, anchor, rel_one, rel_two)
        return scores - lse[0][:, None]

    return jax.shard_map(
        on_device,
        mesh=mesh,
        in_specs=(P("ent", None), P("rep", None), P("rep"), P("rep"), P("rep")),
        out_specs=P("rep", "ent"),
        check_vma=False,
    )
```
